256 devices in a mesh: ctx: 32 (over z, y_hi, core), ch: 8 (over y_lo, x).
Axes of the slice: x: 4, y: 4 (y_hi: 2, y_lo: 2; y = y_hi * 2 + y_lo), z: 8, core: 2. Of those that a mesh axis runs over, the one named last changes fastest.
Arguments:
- query: bfloat16 [16384, 4096], P('ctx', 'ch'), may hold values from -6 to 6
- keys: bfloat16 [16384, 4096], P('ctx', 'ch'), may hold values from -6 to 6
- values: bfloat16 [16384, 4096], P('ctx', 'ch'), may hold values from -6 to 6
- filters: bfloat16 [2048, 4096], P(None, 'ch'), may hold values from -0.125 to 0.125
- segment_ids: int32 [32], P('ctx'), may hold values from 0 to 15, never falling along the last dimension, each value on 1 to 8 neighbouring positions
- out_weight: bfloat16 [4096, 4096], P('ch'), may hold values from -0.125 to 0.125
Outputs:
- mixed_out: bfloat16 [16384, 4096], P('ctx', 'ch')
The draws below stay inside these ranges and needn't reach their ends.
Inputs may be any that keep to these rules, and one draw needn't show every extreme that they name: `segment_ids`: document ids never fall along the sequence; a document covers 1 to 8 whole blocks.
All inputs are finite; a program needn't handle non-finite values.
Results may differ from the reference program's by a relative error of at most 0.024.
Values may be sent and summed in bfloat16 or wider, within the bound.
A program may use at most 128 MiB of HBM per device.

```python
import math
import jax
import jax.numpy as jnp
import numpy as np
from jax import lax

D_WIN = 4096
BLK = 512
FBLK = 4
FL = 2048
SEQ = 16384
DOCS = 16
N_CTX = 32
N_CH = 8


def strengthened(entries, key, source, target, shards_of, factor):
    owner, partner = [(jnp.arange(entries.shape[dim]) // (entries.shape[dim] // shards_of)).reshape([-1 if axis == dim else 1 for axis in range(entries.ndim)]) for dim in (source, target)]
    chosen = jax.random.permutation(key, shards_of)[partner]
    strong = (owner == chosen) | (owner == (partner + shards_of // 2) % shards_of)
    return jnp.where(strong, factor * entries, entries)


def block_scale(stream_key, extent, pieces, smallest, top_value):
    loudness, own = 1.0, jax.random.fold_in(stream_key, 6)
    for axis_at, blocks in pieces:
        draws = jnp.exp(jax.random.uniform(jax.random.fold_in(own, axis_at), (blocks,), jnp.float32, smallest / len(pieces), top_value / len(pieces)))
        loudness = loudness * jnp.repeat(draws, extent[axis_at] // blocks).reshape([-1 if axis == axis_at else 1 for axis in range(len(extent))])
    return loudness


def split_up(amount, total, limit, lean):
    portions = [(1 << 20) // math.isqrt(rank ** lean) + 1 for rank in range(2, amount + 1)]
    surplus, given = total - limit - (amount - 1), [1] * (amount - 1)
    while surplus > 0:
        free = [i for i in range(amount - 1) if given[i] < limit]
        mass, left = sum([portions[i] for i in free]), surplus
        for i in free:
            addition = min(limit - given[i], max(1, left * portions[i] // mass), surplus)
            given[i] = given[i] + addition
            surplus = surplus - addition
    return np.array([limit] + given)


def ragged_sizes(rng, amount, total, reach, lean):
    if amount == 2:
        one = jax.random.randint(rng, (), max(1, total - reach), min(reach, total - 1) + 1)
        return jnp.stack([one, total - one])
    sizes = jnp.asarray(split_up(amount, total, reach, lean), jnp.int32)
    twos = (amount - 1) // 2
    giver, sink = sizes[1:1 + 2 * twos:2], sizes[2:2 + 2 * twos:2]
    room = jnp.minimum(giver - 1, reach - sink)
    moved = jax.random.randint(jax.random.fold_in(rng, 1), (twos,), 0, 1 << 20) % (room + 1)
    sizes = sizes.at[1:1 + 2 * twos:2].set(giver - moved).at[2:2 + 2 * twos:2].set(sink + moved)
    return sizes[jax.random.permutation(jax.random.fold_in(rng, 2), amount)]


def scatter_about(own_key, shape, scale, reach, pieces=(), held_as=jnp.bfloat16):
    loudness = block_scale(own_key, shape, pieces, -0.22, 0.18) if pieces else 1.0
    values = jax.random.normal(own_key, shape, jnp.float32) * scale * loudness
    return jnp.minimum(jnp.maximum(values, -reach), reach).astype(held_as)


def heavy_noise(rng, shape, width, most, cuts, heavy, kind=jnp.bfloat16):
    values = width * jax.random.normal(rng, shape, jnp.float32)
    if cuts:
        values = values * block_scale(rng, shape, cuts, -0.22, 0.18)
    return jnp.clip(strengthened(values, jax.random.fold_in(rng, 3), *heavy), -most, most).astype(kind)


def setup_inputs(seed: int = 0) -> dict:
    key_of = jax.random.split(jax.random.key(seed), 7)
    query = scatter_about(key_of[0], (SEQ, D_WIN), 1.0, 6.0, ((0, 32), (1, 8)))
    keys = scatter_about(key_of[1], (SEQ, D_WIN), 1.0, 6.0, ((0, 32), (1, 8)))
    values = scatter_about(key_of[2], (SEQ, D_WIN), 1.0, 6.0, ((0, 32), (1, 8)))
    filters = scatter_about(key_of[3], (FL, D_WIN), FL ** -0.5, 0.125, ((1, 8),))
    segment_ids = jnp.searchsorted(jnp.cumsum(ragged_sizes(key_of[4], DOCS, N_CTX, 2 * FBLK, 1)), jnp.arange(N_CTX), side="right").astype(jnp.int32)
    out_weight = heavy_noise(key_of[5], (D_WIN, D_WIN), D_WIN ** -0.5, 0.125, ((0, 8),), (0, 1, 8, 2.0))
    return {"query": query, "keys": keys, "values": values, "filters": filters, "segment_ids": segment_ids, "out_weight": out_weight}


def tables(block_len):
    period = 2 * block_len
    frequency = jnp.arange(period, dtype=jnp.int32)[:, None]
    position = jnp.arange(block_len, dtype=jnp.int32)[None, :]
    angles = (2.0 * math.pi / period) * ((frequency * position) % period).astype(jnp.float32)
    forward = jnp.concatenate([jnp.cos(angles), -jnp.sin(angles)], 0).astype(jnp.bfloat16)
    out_rows = jnp.arange(block_len, dtype=jnp.int32)[:, None] + block_len
    freq_cols = jnp.arange(period, dtype=jnp.int32)[None, :]
    angles_back = (2.0 * math.pi / period) * ((out_rows * freq_cols) % period).astype(jnp.float32)
    backward = (jnp.concatenate([jnp.cos(angles_back), -jnp.sin(angles_back)], 1) / period).astype(jnp.bfloat16)
    return forward, backward


def segment_kernels(filters, forward, block_len, reach_blocks):
    period = 2 * block_len
    parity = (1 - 2 * (jnp.arange(period, dtype=jnp.int32) % 2)).astype(jnp.float32)
    parity = jnp.concatenate([parity, parity])[:, None]
    halves = [jnp.dot(forward, filters[offset * block_len:(offset + 1) * block_len], preferred_element_type=jnp.float32) for offset in range(reach_blocks)]
    kernels = []
    for offset in range(reach_blocks + 1):
        current = parity * halves[offset] if offset < reach_blocks else 0.0
        previous = halves[offset - 1] if offset > 0 else 0.0
        kernels.append(previous + current)
    return kernels


def complex_product(spectrum, kernel):
    period = spectrum.shape[0] // 2
    spec_f = spectrum.astype(jnp.float32)
    real_in, imag_in = spec_f[:period], spec_f[period:]
    real_kern, imag_kern = kernel[:period], kernel[period:]
    return jnp.concatenate([real_in * real_kern - imag_in * imag_kern, real_in * imag_kern + imag_in * real_kern], 0)


def reference(query, keys, values, filters, segment_ids, out_weight):
    block_len = BLK
    blocks = SEQ // BLK
    group_width = D_WIN // N_CH
    forward, backward = tables(block_len)
    kernel_stack = jnp.stack(segment_kernels(filters, forward, block_len, FBLK))
    mixed_in = (keys.astype(jnp.float32) * values.astype(jnp.float32)).astype(jnp.bfloat16)
    spectra = lax.map(lambda block_rows: jnp.dot(forward, block_rows, preferred_element_type=jnp.float32).astype(jnp.bfloat16), mixed_in.reshape(blocks, block_len, D_WIN))

    def one_block(block_index):
        own_segment = segment_ids[block_index]
        accumulated = jnp.zeros((4 * block_len, D_WIN), jnp.float32)
        for offset in range(FBLK + 1):
            source = jnp.maximum(block_index - offset, 0).astype(jnp.int32)
            allowed = jnp.logical_and(block_index - offset >= 0, segment_ids[source] == own_segment)
            product = complex_product(spectra[source], kernel_stack[offset])
            accumulated = accumulated + jnp.where(allowed, product, jnp.zeros_like(product))
        filtered = jnp.dot(backward, accumulated.astype(jnp.bfloat16), preferred_element_type=jnp.float32)
        gate_rows = lax.dynamic_slice_in_dim(query, (block_index * block_len).astype(jnp.int32), block_len, 0)
        gated_rows = (gate_rows.astype(jnp.float32) * filtered).astype(jnp.bfloat16)
        total = jnp.zeros((block_len, D_WIN), jnp.float32)
        for group in range(N_CH):
            part = jnp.dot(gated_rows[:, group * group_width:(group + 1) * group_width], out_weight[group * group_width:(group + 1) * group_width], preferred_element_type=jnp.float32)
            total = total + part.astype(jnp.bfloat16).astype(jnp.float32)
        return total.astype(jnp.bfloat16)

    outputs = lax.map(one_block, jnp.arange(blocks, dtype=jnp.int32))
    return outputs.reshape(SEQ, D_WIN)
```

```python
import functools
import math

import jax
import jax.numpy as jnp
import ml_dtypes
import numpy as np
from jax import lax
from jax.experimental import pallas as pl
from jax.experimental.pallas import tpu as pltpu
from jax.sharding import PartitionSpec as P

MESH = pl.DeviceIdType.MESH
BF16, F32 = jnp.bfloat16, jnp.float32

BLK = 512
HALF = 256
NC = BLK // HALF
TAG = 16
ROWS = BLK + TAG
HC = 4
GC = 2
GR = BLK // GC
REACH = 4


def tables():
    period = 2 * BLK
    order = np.concatenate([np.arange(0, BLK, 2), np.arange(1, BLK, 2)])

    def angle(freq, pos):
        return (np.float32(2.0 * math.pi / period) * ((freq * pos) % period).astype(np.float32)).astype(np.float32)

    forward_angles = angle(order[:, None], np.arange(BLK)[None, :])
    real, imag = np.cos(forward_angles), -np.sin(forward_angles)
    imag[0] = np.cos(angle(np.full((1, 1), BLK), np.arange(BLK)[None, :]))[0]
    forward = np.concatenate([real, imag], 0).astype(ml_dtypes.bfloat16)
    out_rows = np.arange(BLK)[:, None] + BLK
    back_angles = angle(out_rows, order[None, :])
    real, imag = 2 * np.cos(back_angles), -2 * np.sin(back_angles)
    real[:, 0] = 1.0
    imag[:, 0] = np.cos(angle(out_rows, np.full((1, 1), BLK)))[:, 0]
    backward = (np.concatenate([real, imag], 1) / np.float32(period)).astype(ml_dtypes.bfloat16)
    return forward, backward


def kernel(seg_ref, q_hbm, k_hbm, v_hbm, filt_hbm, w_hbm, fwd_hbm, bwd_hbm, out_ref,
           q, k, v, filt, fwd, bwd, halo, kern, spec, acc, gated, wts, part, ysend, yrecv, lsem, ssem, rsem):
    ctx, ch = lax.axis_index("ctx"), lax.axis_index("ch")
    z, yh, core = ctx // 4, (ctx // 2) % 2, ctx % 2
    yl, x = ch // 4, ch % 4
    sibling = (z * 4 + yh * 2 + 1 - core, ch)
    y_pair = (ctx, (1 - yl) * 4 + x)
    y_far = (z * 4 + (1 - yh) * 2 + core, ch)
    z_next, z_prev = (((z + 1) % 8) * 4 + yh * 2 + core, ch), (((z + 7) % 8) * 4 + yh * 2 + core, ch)
    x_next, x_prev = (ctx, yl * 4 + (x + 1) % 4), (ctx, yl * 4 + (x + 3) % 4)
    x_far = (ctx, yl * 4 + (x + 2) % 4)

    barrier = pltpu.get_barrier_semaphore()
    for device in (sibling, y_pair, y_far, z_prev, x_next, x_prev, x_far):
        pl.semaphore_signal(barrier, inc=1, device_id=device, device_id_type=MESH)

    counter = [0]
    pending = []

    def number():
        counter[0] += 1
        return counter[0] - 1

    def remote(src, dst, sem, device):
        return pltpu.make_async_remote_copy(src_ref=src, dst_ref=dst, send_sem=ssem.at[sem], recv_sem=rsem.at[sem],
                                            device_id=device, device_id_type=MESH)

    def send(src, dst, device):
        copy = remote(src, dst, number(), device)
        copy.start()
        pending.append(copy)
        return copy

    local_count = [0]

    def load(src, dst):
        copy = pltpu.make_async_copy(src, dst, lsem.at[local_count[0]])
        local_count[0] += 1
        copy.start()
        return copy

    X, A, Y, B, Z = 0, 1, 2, 3, 4
    lanes = [pl.ds(c * HALF, HALF) for c in range(NC)]
    kv = [(load(k_hbm.at[:, lanes[c]], k.at[c]), load(v_hbm.at[:, lanes[c]], v.at[c])) for c in range(NC)]
    load_fwd = load(fwd_hbm, fwd)
    load_filt = [load(filt_hbm.at[:, lanes[c]], filt.at[c]) for c in range(NC)]
    load_bwd = load(bwd_hbm, bwd)
    load_q = [load(q_hbm.at[:, lanes[c]], q.at[c]) for c in range(NC)]

    def columns(r, xx):
        yy = yl if r == 0 else 1 - yl
        return pl.ds(pl.multiple_of((yy * 4 + xx) * BLK, BLK), BLK)

    load_w = [load(w_hbm.at[:, columns(r, x)], wts.at[0, :, pl.ds(r * BLK, BLK)]) for r in range(2)]

    tag = jnp.full((TAG, HALF), seg_ref[0].astype(F32)).astype(BF16)
    for c in range(NC):
        for copy in kv[c]:
            copy.wait()
        halo[X, c, pl.ds(0, BLK)] = (k[c].astype(F32) * v[c].astype(F32)).astype(BF16)
        halo[X, c, pl.ds(BLK, TAG)] = tag
    pl.semaphore_wait(barrier, 7)

    piece = BLK // HC
    pieces = [pl.ds(p * piece, piece + (TAG if p == HC - 1 else 0)) for p in range(HC)]
    z_copies, y_sems, s_sems = {}, {}, {}
    for c in range(NC):
        for p in range(HC):
            z_copies[c, p] = send(halo.at[X, c, pieces[p]], halo.at[Z, c, pieces[p]], z_next)
            y_sems[c, p] = number()
            own = remote(halo.at[X, c, pieces[p]], halo.at[Y, c, pieces[p]], y_sems[c, p], y_far)
            pending.append(own)

            @pl.when(yh == 0)
            def _():
                own.start()
        for slot in (A, B):
            s_sems[slot, c] = number()
        first = remote(halo.at[X, c], halo.at[A, c], s_sems[A, c], sibling)
        pending.append(first)

        @pl.when(core == 0)
        def _():
            first.start()

    half_rows = pl.ds(pl.multiple_of(core * HALF, HALF), HALF)
    w_copies = {}
    for slot, device, xx in ((1, x_next, (x + 1) % 4), (2, x_prev, (x + 3) % 4), (3, x_far, (x + 2) % 4)):
        for r in range(2):
            w_copies[slot, r] = send(w_hbm.at[half_rows, columns(r, xx)],
                                     wts.at[slot, half_rows, pl.ds(r * BLK, BLK)], device)

    def relay(c, p):
        @pl.when(yh == 1)
        def _():
            z_copies[c, p].wait_recv()
            remote(halo.at[Z, c, pieces[p]], halo.at[Y, c, pieces[p]], y_sems[c, p], y_far).start()

    def share(c):
        @pl.when(yh == 0)
        def _():
            for p in range(HC):
                z_copies[c, p].wait_recv()
        for p in range(HC):
            remote(halo.at[X, c, pieces[p]], halo.at[Y, c, pieces[p]], y_sems[c, p], y_far).wait_recv()

        @pl.when(core == 0)
        def _():
            remote(halo.at[Y, c], halo.at[B, c], s_sems[B, c], sibling).start()

        @pl.when(core == 1)
        def _():
            remote(halo.at[Y, c], halo.at[A, c], s_sems[A, c], sibling).start()
            remote(halo.at[Z, c], halo.at[B, c], s_sems[B, c], sibling).start()
        pending.append(remote(halo.at[Y, c], halo.at[B, c], s_sems[B, c], sibling))

    def quarter(g):
        return pl.ds(pl.multiple_of(g * HALF, HALF), HALF)

    def filter_kernels(c, d):
        taps = filt[c, pl.ds(d * BLK, BLK), :]

        @pl.loop(0, 4)
        def _(g):
            part_g = jnp.dot(fwd[quarter(g)], taps, preferred_element_type=F32)
            sign = (1 - 2 * (g % 2)).astype(F32)
            if d == 0:
                kern[0, c, quarter(g)] = sign * part_g
            else:
                kern[d, c, quarter(g)] += sign * part_g
            kern[d + 1, c, quarter(g)] = part_g

    def spectrum(c, d):
        block = halo[d, c, pl.ds(0, BLK)]
        if d:
            same = halo[d, c, pl.ds(BLK, TAG)].astype(F32)[0:1] == seg_ref[0].astype(F32)
            keep = jnp.where(jnp.logical_and(same, ctx >= d), 1.0, 0.0)

        @pl.loop(0, 4)
        def _(g):
            value = jnp.dot(fwd[quarter(g)], block, preferred_element_type=F32)
            spec[d, quarter(g)] = value * keep if d else value

    def product(c):
        def rows_at(start, rows, first):
            re_rows, im_rows = pl.ds(start, rows), pl.ds(start + BLK, rows)
            re, im = 0.0, 0.0
            if first:
                zeroth = lax.broadcasted_iota(jnp.int32, (rows, HALF), 0) == 0
            for d in range(REACH + 1):
                a_r, a_i = spec[d, re_rows], spec[d, im_rows]
                g_r, g_i = kern[d, c, re_rows], kern[d, c, im_rows]
                rr, ii, ri, ir = a_r * g_r, a_i * g_i, a_r * g_i, a_i * g_r
                if first:
                    re = re + (rr - jnp.where(zeroth, 0.0, ii))
                    im = im + jnp.where(zeroth, ii, ri + ir)
                else:
                    re = re + (rr - ii)
                    im = im + (ri + ir)
            acc[re_rows] = re.astype(BF16)
            acc[im_rows] = im.astype(BF16)

        rows_at(0, 16, True)

        @pl.loop(1, BLK // 16, unroll=1)
        def _(step):
            rows_at(pl.multiple_of(step * 16, 16), 16, False)

    g_copies = {}

    def gate(c, r):
        rows = pl.ds(r * GR, GR)
        value = jnp.dot(bwd[rows], acc[...], preferred_element_type=F32)
        gated[0, c, rows] = (q[c, rows].astype(F32) * value).astype(BF16)
        g_copies[1, c, r] = send(gated.at[0, c, rows], gated.at[1, c, rows], x_next)
        g_copies[2, c, r] = send(gated.at[0, c, rows], gated.at[2, c, rows], x_prev)

    def pass_on(c, r):
        low, high = pl.ds(r * GR, GR // 2), pl.ds(r * GR + GR // 2, GR // 2)
        g_copies[1, c, r].wait_recv()
        g_copies[3, c, r, 0] = send(gated.at[1, c, low], gated.at[3, c, low], x_next)
        g_copies[2, c, r].wait_recv()
        g_copies[3, c, r, 1] = send(gated.at[2, c, high], gated.at[3, c, high], x_prev)

    load_fwd.wait()
    load_filt[0].wait()
    for d in range(REACH):
        filter_kernels(0, d)
    spectrum(0, X)
    load_filt[1].wait()
    for p in range(HC):
        relay(0, p)
        filter_kernels(1, p)
    share(0)
    load_bwd.wait()
    load_q[0].wait()
    load_q[1].wait()

    for c in range(NC):
        spectrum(c, Y) if c == 0 else spectrum(c, X)
        if c == 0:
            relay(1, 0)
        else:
            spectrum(c, Y)
        spectrum(c, Z)
        if c == 0:
            relay(1, 1)
        for slot in (A, B):
            remote(halo.at[Y, c], halo.at[slot, c], s_sems[slot, c], sibling).wait_recv()
            spectrum(c, slot)
            if c == 0:
                relay(1, 2 if slot == A else 3)
        product(c)
        for r in range(GC):
            gate(c, r)
        if c == 0:
            share(1)

    for c in range(NC):
        for r in range(GC):
            pass_on(c, r)

    s_w = {}

    def weights_arrive(slot):
        for r in range(2):
            w_copies[slot, r].wait_recv()
        s_w[slot] = send(wts.at[slot, half_rows], wts.at[slot, half_rows], sibling)

    def project(slot, c, r, fresh):
        rows = pl.ds(r * GR, GR)

        @pl.loop(0, 4)
        def _(n):
            cols = quarter(n)
            value = jnp.dot(gated[slot, c, rows], wts[slot, pl.ds(c * HALF, HALF), cols], preferred_element_type=F32)
            if fresh:
                part[rows, cols] = value
            else:
                part[rows, cols] += value

    for copy in load_w:
        copy.wait()
    for c in range(NC):
        for r in range(GC):
            project(0, c, r, c == 0)
    for slot in (1, 2):
        weights_arrive(slot)
        s_w[slot].wait_recv()
        for c in range(NC):
            for r in range(GC):
                project(slot, c, r, False)
    weights_arrive(3)
    s_w[3].wait_recv()
    y_copies = []
    for r in range(GC):
        rows = pl.ds(r * GR, GR)
        for c in range(NC):
            for side in range(2):
                g_copies[3, c, r, side].wait_recv()
            project(3, c, r, False)
        ysend[rows] = part[rows, pl.ds(BLK, BLK)].astype(BF16)
        y_copies.append(send(ysend.at[rows], yrecv.at[rows], y_pair))
    for r in range(GC):
        rows = pl.ds(r * GR, GR)
        y_copies[r].wait_recv()
        out_ref[rows] = (part[rows, pl.ds(0, BLK)] + yrecv[rows].astype(F32)).astype(BF16)
    for copy in pending:
        copy.wait_send()


def on_device(query, keys, values, filters, segment_ids, out_weight):
    forward, backward = tables()
    anywhere = pl.BlockSpec(memory_space=pl.ANY)
    return pl.pallas_call(
        kernel,
        out_shape=jax.ShapeDtypeStruct((BLK, BLK), BF16),
        in_specs=[pl.BlockSpec(memory_space=pltpu.SMEM)] + [anywhere] * 7,
        out_specs=pl.BlockSpec(memory_space=pltpu.VMEM),
        scratch_shapes=[
            pltpu.VMEM((NC, BLK, HALF), BF16),
            pltpu.VMEM((NC, BLK, HALF), BF16),
            pltpu.VMEM((NC, BLK, HALF), BF16),
            pltpu.VMEM((NC, REACH * BLK, HALF), BF16),
            pltpu.VMEM((2 * BLK, BLK), BF16),
            pltpu.VMEM((BLK, 2 * BLK), BF16),
            pltpu.VMEM((REACH + 1, NC, ROWS, HALF), BF16),
            pltpu.VMEM((REACH + 1, NC, 2 * BLK, HALF), F32),
            pltpu.VMEM((REACH + 1, 2 * BLK, HALF), F32),
            pltpu.VMEM((2 * BLK, HALF), BF16),
            pltpu.VMEM((4, NC, BLK, HALF), BF16),
            pltpu.VMEM((4, BLK, 2 * BLK), BF16),
            pltpu.VMEM((BLK, 2 * BLK), F32),
            pltpu.VMEM((BLK, BLK), BF16),
            pltpu.VMEM((BLK, BLK), BF16),
            pltpu.SemaphoreType.DMA((16,)),
            pltpu.SemaphoreType.DMA((64,)),
            pltpu.SemaphoreType.DMA((64,)),
        ],
        compiler_params=pltpu.CompilerParams(collective_id=0, has_side_effects=True, vmem_limit_bytes=56 * 2**20),
        name="hyena",
    )(segment_ids, query, keys, values, filters, out_weight, jnp.asarray(forward), jnp.asarray(backward))


def solution(mesh):
    in_specs = (
        P("ctx", "ch"),
        P("ctx", "ch"),
        P("ctx", "ch"),
        P(None, "ch"),
        P("ctx"),
        P("ch", None),
    )
    return jax.shard_map(on_device, mesh=mesh, in_specs=in_specs, out_specs=P("ctx", "ch"), check_vma=False)
```

```python
import functools
import math

import jax
import jax.numpy as jnp
import ml_dtypes
import numpy as np
from jax import lax
from jax.experimental import pallas as pl
from jax.experimental.pallas import tpu as pltpu
from jax.sharding import PartitionSpec as P

MESH = pl.DeviceIdType.MESH
BF16, F32 = jnp.bfloat16, jnp.float32

BLK = 512
HALF = 256
NC = BLK // HALF
TAG = 16
ROWS = BLK + TAG
HC = 4
GC = 4
GR = BLK // GC
QUARTER = BLK // 4
REACH = 4


def tables():
    period = 2 * BLK
    order = np.concatenate([np.arange(0, BLK, 2), np.arange(1, BLK, 2)])

    def angle(freq, pos):
        return (np.float32(2.0 * math.pi / period) * ((freq * pos) % period).astype(np.float32)).astype(np.float32)

    forward_angles = angle(order[:, None], np.arange(BLK)[None, :])
    real, imag = np.cos(forward_angles), -np.sin(forward_angles)
    imag[0] = np.cos(angle(np.full((1, 1), BLK), np.arange(BLK)[None, :]))[0]
    forward = np.concatenate([real, imag], 0).astype(ml_dtypes.bfloat16)
    out_rows = np.arange(BLK)[:, None] + BLK
    back_angles = angle(out_rows, order[None, :])
    real, imag = 2 * np.cos(back_angles), -2 * np.sin(back_angles)
    real[:, 0] = 1.0
    imag[:, 0] = np.cos(angle(out_rows, np.full((1, 1), BLK)))[:, 0]
    backward = (np.concatenate([real, imag], 1) / np.float32(period)).astype(ml_dtypes.bfloat16)
    return forward, backward


def kernel(seg_ref, q_hbm, k_hbm, v_hbm, filt_hbm, w_hbm, fwd_hbm, bwd_hbm, out_ref,
           q, k, v, filt, fwd, bwd, halo, kern, spec, acc, gated, wts, part, ysend, yrecv, lsem, ssem, rsem):
    ctx, ch = lax.axis_index("ctx"), lax.axis_index("ch")
    z, yh, core = ctx // 4, (ctx // 2) % 2, ctx % 2
    yl, x = ch // 4, ch % 4
    zpar = z % 2
    sibling = (z * 4 + yh * 2 + 1 - core, ch)
    y_pair = (ctx, (1 - yl) * 4 + x)
    y_far = (z * 4 + (1 - yh) * 2 + core, ch)
    z_next, z_prev = (((z + 1) % 8) * 4 + yh * 2 + core, ch), (((z + 7) % 8) * 4 + yh * 2 + core, ch)
    z_pair = ((z + 1 - 2 * zpar) * 4 + yh * 2 + core, ch)
    x_next, x_prev = (ctx, yl * 4 + (x + 1) % 4), (ctx, yl * 4 + (x + 3) % 4)
    x_far = (ctx, yl * 4 + (x + 2) % 4)
    first_z, last_z = z == 0, z == 7

    def signal(device):
        pl.semaphore_signal(barrier, inc=1, device_id=device, device_id_type=MESH)

    barrier = pltpu.get_barrier_semaphore()
    for device in (sibling, y_pair, y_far, x_next, x_prev, x_far):
        signal(device)

    @pl.when(jnp.logical_not(first_z))
    def _():
        signal(z_prev)

    @pl.when(jnp.logical_not(last_z))
    def _():
        signal(z_next)

    counter = [0, 0]
    always, by_condition = [], []

    def number():
        counter[0] += 1
        return counter[0] - 1

    def remote(src, dst, sem, device):
        return pltpu.make_async_remote_copy(src_ref=src, dst_ref=dst, send_sem=ssem.at[sem], recv_sem=rsem.at[sem],
                                            device_id=device, device_id_type=MESH)

    def send(src, dst, device):
        copy = remote(src, dst, number(), device)
        copy.start()
        always.append(copy)
        return copy

    def load(src, dst):
        copy = pltpu.make_async_copy(src, dst, lsem.at[counter[1]])
        counter[1] += 1
        copy.start()
        return copy

    X, A, Y, B, Z = 0, 1, 2, 3, 4
    lanes = [pl.ds(c * HALF, HALF) for c in range(NC)]
    kv = [(load(k_hbm.at[:, lanes[c]], k.at[c]), load(v_hbm.at[:, lanes[c]], v.at[c])) for c in range(NC)]
    load_fwd = load(fwd_hbm, fwd)
    load_filt = [load(filt_hbm.at[:, lanes[c]], filt.at[c]) for c in range(NC)]
    load_bwd = load(bwd_hbm, bwd)
    load_q = [load(q_hbm.at[:, lanes[c]], q.at[c]) for c in range(NC)]

    def columns(r, xx):
        yy = yl if r == 0 else 1 - yl
        return pl.ds(pl.multiple_of((yy * 4 + xx) * BLK, BLK), BLK)

    load_w = [load(w_hbm.at[pl.ds(c * HALF, HALF), columns(r, x)], wts.at[c, pl.ds(0, HALF), pl.ds(r * BLK, BLK)])
              for c in range(NC) for r in range(2)]

    @pl.when(first_z)
    def _():
        halo[Z] = jnp.zeros((NC, ROWS, HALF), BF16)

        @pl.when(yh == 0)
        def _():
            halo[Y] = jnp.zeros((NC, ROWS, HALF), BF16)

    tag = jnp.full((TAG, HALF), seg_ref[0].astype(F32)).astype(BF16)
    for c in range(NC):
        for copy in kv[c]:
            copy.wait()
        halo[X, c, pl.ds(0, BLK)] = (k[c].astype(F32) * v[c].astype(F32)).astype(BF16)
        halo[X, c, pl.ds(BLK, TAG)] = tag
    pl.semaphore_wait(barrier, 8 - first_z.astype(jnp.int32) - last_z.astype(jnp.int32))

    piece = BLK // HC
    pieces = [pl.ds(p * piece, piece + (TAG if p == HC - 1 else 0)) for p in range(HC)]
    z_copies, y_copies, s_copies, s_sems = {}, {}, {}, {}
    gets_y = jnp.logical_or(yh == 1, jnp.logical_not(first_z))
    gives_y = jnp.logical_or(yh == 0, jnp.logical_not(first_z))
    for c in range(NC):
        for p, rows in enumerate(pieces):
            z_copies[c, p] = remote(halo.at[X, c, rows], halo.at[Z, c, rows], number(), z_next)
            y_copies[c, p] = [remote(halo.at[src, c, rows], halo.at[Y, c, rows], counter[0], y_far) for src in (X, Z)]
            number()
            s_sems[A, c, p], s_sems[B, c, p] = number(), number()
            by_condition.append((jnp.logical_not(last_z), z_copies[c, p]))
            by_condition.append((gives_y, y_copies[c, p][0]))
            for slot in (A, B):
                s_copies[slot, c, p] = remote(halo.at[X, c, rows], halo.at[slot, c, rows], s_sems[slot, c, p], sibling)
                always.append(s_copies[slot, c, p])

            @pl.when(jnp.logical_not(last_z))
            def _():
                z_copies[c, p].start()

            @pl.when(yh == 0)
            def _():
                y_copies[c, p][0].start()

            @pl.when(core == 0)
            def _():
                s_copies[A, c, p].start()

    w_copies, w_z, w_sib = {}, {}, {}

    def w_rows(slot, parity):
        return pl.ds(pl.multiple_of(slot * HALF + parity * QUARTER, QUARTER), QUARTER)

    own_rows = pl.ds(pl.multiple_of(core * HALF + zpar * QUARTER, QUARTER), QUARTER)
    for slot, device, xx in ((1, x_next, (x + 1) % 4), (2, x_prev, (x + 3) % 4), (3, x_far, (x + 2) % 4)):
        for r in range(2):
            w_copies[slot, r] = send(w_hbm.at[own_rows, columns(r, xx)],
                                     wts.at[core, w_rows(slot, zpar), pl.ds(r * BLK, BLK)], device)

    def weights_on(slot):
        for r in range(2):
            w_copies[slot, r].wait_recv()
        mine = wts.at[core, w_rows(slot, zpar)]
        w_z[slot] = send(mine, mine, z_pair)
        w_sib[slot, 0] = send(mine, mine, sibling)

    def weights_share(slot):
        w_z[slot].wait_recv()
        theirs = wts.at[core, w_rows(slot, 1 - zpar)]
        w_sib[slot, 1] = send(theirs, theirs, sibling)

    def weights_wait(slot):
        for part_of in range(2):
            w_sib[slot, part_of].wait_recv()

    def z_arrives(c, p):
        rows = pieces[p]

        @pl.when(jnp.logical_not(first_z))
        def _():
            z_copies[c, p].wait_recv()

            @pl.when(yh == 1)
            def _():
                y_copies[c, p][1].start()

        @pl.when(core == 1)
        def _():
            remote(halo.at[Z, c, rows], halo.at[B, c, rows], s_sems[B, c, p], sibling).start()

    def y_arrives(c, p):
        rows = pieces[p]

        @pl.when(gets_y)
        def _():
            y_copies[c, p][0].wait_recv()

        @pl.when(core == 0)
        def _():
            remote(halo.at[Y, c, rows], halo.at[B, c, rows], s_sems[B, c, p], sibling).start()

        @pl.when(core == 1)
        def _():
            remote(halo.at[Y, c, rows], halo.at[A, c, rows], s_sems[A, c, p], sibling).start()

    def shared(c, slot):
        for p in range(HC):
            s_copies[slot, c, p].wait_recv()

    even_odd = [pl.ds(g * HALF, HALF) for g in range(4)]

    def filter_kernels(c, d):
        taps = filt[c, pl.ds(d * BLK, BLK), :]
        for g, rows in enumerate(even_odd):
            part_g = jnp.dot(fwd[rows], taps, preferred_element_type=F32)
            turned = -part_g if g % 2 else part_g
            kern[d, c, rows] = kern[d, c, rows] + turned if d else turned
            kern[d + 1, c, rows] = part_g

    def spectrum(c, d):
        block = halo[d, c, pl.ds(0, BLK)]
        if d:
            same = halo[d, c, pl.ds(BLK, TAG)].astype(F32)[0:1] == seg_ref[0].astype(F32)
            keep = jnp.where(jnp.logical_and(same, ctx >= d), 1.0, 0.0)
        for rows in even_odd:
            value = jnp.dot(fwd[rows], block, preferred_element_type=F32)
            spec[d, rows] = value * keep if d else value

    def product(c):
        def rows_at(start, rows, first):
            re_rows, im_rows = pl.ds(start, rows), pl.ds(start + BLK, rows)
            re, im = 0.0, 0.0
            if first:
                zeroth = lax.broadcasted_iota(jnp.int32, (rows, HALF), 0) == 0
            for d in range(REACH + 1):
                a_r, a_i = spec[d, re_rows], spec[d, im_rows]
                g_r, g_i = kern[d, c, re_rows], kern[d, c, im_rows]
                rr, ii, ri, ir = a_r * g_r, a_i * g_i, a_r * g_i, a_i * g_r
                if first:
                    re = re + (rr - jnp.where(zeroth, 0.0, ii))
                    im = im + jnp.where(zeroth, ii, ri + ir)
                else:
                    re = re + (rr - ii)
                    im = im + (ri + ir)
            acc[re_rows] = re.astype(BF16)
            acc[im_rows] = im.astype(BF16)

        @pl.loop(0, BLK // 64)
        def _(step):
            for u in range(4):
                rows_at(pl.multiple_of(step * 64 + u * 16, 16), 16, False)

        rows_at(0, 16, True)

    g_copies = {}

    def slot_lanes(slot):
        return pl.ds(slot * HALF, HALF)

    def gate(c, r):
        rows = pl.ds(r * GR, GR)
        value = jnp.dot(bwd[rows], acc[...], preferred_element_type=F32)
        gated[c, rows, slot_lanes(0)] = (q[c, rows].astype(F32) * value).astype(BF16)
        own = gated.at[c, rows, slot_lanes(0)]
        g_copies[1, c, r] = send(own, gated.at[c, rows, slot_lanes(1)], x_next)
        g_copies[2, c, r] = send(own, gated.at[c, rows, slot_lanes(2)], x_prev)

    def pass_on(c, r):
        low, high = pl.ds(r * GR, GR // 2), pl.ds(r * GR + GR // 2, GR // 2)
        for slot, rows, device in ((1, low, x_next), (2, high, x_prev)):
            g_copies[slot, c, r].wait_recv()
            g_copies[3, c, r, slot] = send(gated.at[c, rows, slot_lanes(slot)], gated.at[c, rows, slot_lanes(3)], device)

    def gathered(c, r):
        for slot in (1, 2):
            g_copies[3, c, r, slot].wait_recv()

    load_fwd.wait()
    load_filt[0].wait()
    spectrum(0, X)
    for d in range(REACH):
        filter_kernels(0, d)
    load_filt[1].wait()
    for p in range(HC):
        z_arrives(0, p)
        filter_kernels(1, p)
    load_bwd.wait()
    load_q[0].wait()
    load_q[1].wait()
    for p in range(HC):
        y_arrives(0, p)
    spectrum(0, Z)
    z_arrives(1, 0)
    spectrum(0, Y)
    z_arrives(1, 1)
    shared(0, A)
    spectrum(0, A)
    z_arrives(1, 2)
    shared(0, B)
    spectrum(0, B)
    z_arrives(1, 3)
    product(0)
    for r in range(GC):
        gate(0, r)
    weights_on(1)
    weights_on(2)
    spectrum(1, X)
    for p in range(HC):
        y_arrives(1, p)
    spectrum(1, Z)
    spectrum(1, Y)
    shared(1, A)
    spectrum(1, A)
    shared(1, B)
    spectrum(1, B)
    product(1)
    for r in range(GC):
        gate(1, r)
    weights_on(3)

    own_cols, other_cols = pl.ds(0, BLK), pl.ds(BLK, BLK)

    def project(c, rows, cols):
        return jnp.dot(gated[c, rows], wts[c, :, cols], preferred_element_type=F32)

    for r in range(GC):
        pass_on(0, r)
    for copy in load_w:
        copy.wait()
    for slot in (1, 2, 3):
        weights_share(slot)
    for r in range(GC):
        pass_on(1, r)
    for slot in (1, 2, 3):
        weights_wait(slot)
    for r in range(GC):
        gathered(0, r)
    everything = pl.ds(0, BLK)
    for cols in (other_cols, own_cols):
        part[:, cols] = project(0, everything, cols)
    swaps = []
    for r in range(GC):
        rows = pl.ds(r * GR, GR)
        gathered(1, r)
        ysend[rows] = (part[rows, other_cols] + project(1, rows, other_cols)).astype(BF16)
        swaps.append(send(ysend.at[rows], yrecv.at[rows], y_pair))
    part[:, own_cols] += project(1, everything, own_cols)
    for r in range(GC):
        rows = pl.ds(r * GR, GR)
        swaps[r].wait_recv()
        out_ref[rows] = (part[rows, own_cols] + yrecv[rows].astype(F32)).astype(BF16)
    for copy in always:
        copy.wait_send()
    for condition, copy in by_condition:
        @pl.when(condition)
        def _():
            copy.wait_send()


def on_device(query, keys, values, filters, segment_ids, out_weight):
    forward, backward = tables()
    anywhere = pl.BlockSpec(memory_space=pl.ANY)
    return pl.pallas_call(
        kernel,
        out_shape=jax.ShapeDtypeStruct((BLK, BLK), BF16),
        in_specs=[pl.BlockSpec(memory_space=pltpu.SMEM)] + [anywhere] * 7,
        out_specs=pl.BlockSpec(memory_space=pltpu.VMEM),
        scratch_shapes=[
            pltpu.VMEM((NC, BLK, HALF), BF16),
            pltpu.VMEM((NC, BLK, HALF), BF16),
            pltpu.VMEM((NC, BLK, HALF), BF16),
            pltpu.VMEM((NC, REACH * BLK, HALF), BF16),
            pltpu.VMEM((2 * BLK, BLK), BF16),
            pltpu.VMEM((BLK, 2 * BLK), BF16),
            pltpu.VMEM((REACH + 1, NC, ROWS, HALF), BF16),
            pltpu.VMEM((REACH + 1, NC, 2 * BLK, HALF), F32),
            pltpu.VMEM((REACH + 1, 2 * BLK, HALF), F32),
            pltpu.VMEM((2 * BLK, HALF), BF16),
            pltpu.VMEM((NC, BLK, 4 * HALF), BF16),
            pltpu.VMEM((NC, 4 * HALF, 2 * BLK), BF16),
            pltpu.VMEM((BLK, 2 * BLK), F32),
            pltpu.VMEM((BLK, BLK), BF16),
            pltpu.VMEM((BLK, BLK), BF16),
            pltpu.SemaphoreType.DMA((16,)),
            pltpu.SemaphoreType.DMA((96,)),
            pltpu.SemaphoreType.DMA((96,)),
        ],
        compiler_params=pltpu.CompilerParams(collective_id=0, has_side_effects=True, vmem_limit_bytes=56 * 2**20),
        name="hyena",
    )(segment_ids, query, keys, values, filters, out_weight, jnp.asarray(forward), jnp.asarray(backward))


def solution(mesh):
    in_specs = (
        P("ctx", "ch"),
        P("ctx", "ch"),
        P("ctx", "ch"),
        P(None, "ch"),
        P("ctx"),
        P("ch", None),
    )
    return jax.shard_map(on_device, mesh=mesh, in_specs=in_specs, out_specs=P("ctx", "ch"), check_vma=False)
```

```python
import functools
import math

import jax
import jax.numpy as jnp
import ml_dtypes
import numpy as np
from jax import lax
from jax.experimental import pallas as pl
from jax.experimental.pallas import tpu as pltpu
from jax.sharding import PartitionSpec as P

MESH = pl.DeviceIdType.MESH
BF16, F32 = jnp.bfloat16, jnp.float32

BLK = 512
HALF = 256
NC = BLK // HALF
TAG = 16
ROWS = BLK + TAG
HC = 4
GC = 4
GR = BLK // GC
QUARTER = BLK // 4
REACH = 4


def tables():
    period = 2 * BLK
    order = np.concatenate([np.arange(0, BLK, 2), np.arange(1, BLK, 2)])

    def angle(freq, pos):
        return (np.float32(2.0 * math.pi / period) * ((freq * pos) % period).astype(np.float32)).astype(np.float32)

    forward_angles = angle(order[:, None], np.arange(BLK)[None, :])
    real, imag = np.cos(forward_angles), -np.sin(forward_angles)
    imag[0] = np.cos(angle(np.full((1, 1), BLK), np.arange(BLK)[None, :]))[0]
    forward = np.concatenate([real, imag], 0).astype(ml_dtypes.bfloat16)
    out_rows = np.arange(BLK)[:, None] + BLK
    back_angles = angle(out_rows, order[None, :])
    real, imag = 2 * np.cos(back_angles), -2 * np.sin(back_angles)
    real[:, 0] = 1.0
    imag[:, 0] = np.cos(angle(out_rows, np.full((1, 1), BLK)))[:, 0]
    backward = (np.concatenate([real, imag], 1) / np.float32(period)).astype(ml_dtypes.bfloat16)
    return forward, backward


def kernel(seg_ref, q_hbm, k_hbm, v_hbm, filt_hbm, w_hbm, fwd_hbm, bwd_hbm, out_ref,
           q, k, v, filt, fwd, bwd, halo, kern, spec, acc, gated, wts, part, ysend, yrecv, lsem, ssem, rsem):
    ctx, ch = lax.axis_index("ctx"), lax.axis_index("ch")
    z, yh, core = ctx // 4, (ctx // 2) % 2, ctx % 2
    yl, x = ch // 4, ch % 4
    zpar = z % 2
    sibling = (z * 4 + yh * 2 + 1 - core, ch)
    y_pair = (ctx, (1 - yl) * 4 + x)
    y_far = (z * 4 + (1 - yh) * 2 + core, ch)
    z_next, z_prev = (((z + 1) % 8) * 4 + yh * 2 + core, ch), (((z + 7) % 8) * 4 + yh * 2 + core, ch)
    z_pair = ((z + 1 - 2 * zpar) * 4 + yh * 2 + core, ch)
    x_next, x_prev = (ctx, yl * 4 + (x + 1) % 4), (ctx, yl * 4 + (x + 3) % 4)
    x_far = (ctx, yl * 4 + (x + 2) % 4)
    first_z, last_z = z == 0, z == 7

    def signal(device):
        pl.semaphore_signal(barrier, inc=1, device_id=device, device_id_type=MESH)

    barrier = pltpu.get_barrier_semaphore()
    for device in (sibling, y_pair, y_far, x_next, x_prev, x_far):
        signal(device)

    @pl.when(jnp.logical_not(first_z))
    def _():
        signal(z_prev)

    @pl.when(jnp.logical_not(last_z))
    def _():
        signal(z_next)

    counter = [0, 0]
    always, by_condition = [], []

    def number():
        counter[0] += 1
        return counter[0] - 1

    def remote(src, dst, sem, device):
        return pltpu.make_async_remote_copy(src_ref=src, dst_ref=dst, send_sem=ssem.at[sem], recv_sem=rsem.at[sem],
                                            device_id=device, device_id_type=MESH)

    def send(src, dst, device):
        copy = remote(src, dst, number(), device)
        copy.start()
        always.append(copy)
        return copy

    def load(src, dst):
        copy = pltpu.make_async_copy(src, dst, lsem.at[counter[1]])
        counter[1] += 1
        copy.start()
        return copy

    X, A, Y, B, Z = 0, 1, 2, 3, 4
    lanes = [pl.ds(c * HALF, HALF) for c in range(NC)]
    kv = [(load(k_hbm.at[:, lanes[c]], k.at[c]), load(v_hbm.at[:, lanes[c]], v.at[c])) for c in range(NC)]
    load_fwd = load(fwd_hbm, fwd)
    load_filt = [load(filt_hbm.at[:, lanes[c]], filt.at[c]) for c in range(NC)]
    load_bwd = load(bwd_hbm, bwd)
    load_q = [load(q_hbm.at[:, lanes[c]], q.at[c]) for c in range(NC)]

    def columns(r, xx):
        yy = yl if r == 0 else 1 - yl
        return pl.ds(pl.multiple_of((yy * 4 + xx) * BLK, BLK), BLK)

    load_w = [load(w_hbm.at[pl.ds(c * HALF, HALF), columns(r, x)], wts.at[c, pl.ds(0, HALF), pl.ds(r * BLK, BLK)])
              for c in range(NC) for r in range(2)]

    @pl.when(first_z)
    def _():
        halo[Z] = jnp.zeros((NC, ROWS, HALF), BF16)

        @pl.when(yh == 0)
        def _():
            halo[Y] = jnp.zeros((NC, ROWS, HALF), BF16)

    tag = jnp.full((TAG, HALF), seg_ref[0].astype(F32)).astype(BF16)
    for c in range(NC):
        for copy in kv[c]:
            copy.wait()
        halo[X, c, pl.ds(0, BLK)] = (k[c].astype(F32) * v[c].astype(F32)).astype(BF16)
        halo[X, c, pl.ds(BLK, TAG)] = tag
    pl.semaphore_wait(barrier, 8 - first_z.astype(jnp.int32) - last_z.astype(jnp.int32))

    piece = BLK // HC
    pieces = [pl.ds(p * piece, piece + (TAG if p == HC - 1 else 0)) for p in range(HC)]
    z_copies, y_copies, s_copies, s_sems = {}, {}, {}, {}
    gets_y = jnp.logical_or(yh == 1, jnp.logical_not(first_z))
    gives_y = jnp.logical_or(yh == 0, jnp.logical_not(first_z))
    for c in range(NC):
        for p, rows in enumerate(pieces):
            z_copies[c, p] = remote(halo.at[X, c, rows], halo.at[Z, c, rows], number(), z_next)
            y_copies[c, p] = [remote(halo.at[src, c, rows], halo.at[Y, c, rows], counter[0], y_far) for src in (X, Z)]
            number()
            s_sems[A, c, p], s_sems[B, c, p] = number(), number()
            by_condition.append((jnp.logical_not(last_z), z_copies[c, p]))
            by_condition.append((gives_y, y_copies[c, p][0]))
            for slot in (A, B):
                s_copies[slot, c, p] = remote(halo.at[X, c, rows], halo.at[slot, c, rows], s_sems[slot, c, p], sibling)
                always.append(s_copies[slot, c, p])

            @pl.when(jnp.logical_not(last_z))
            def _():
                z_copies[c, p].start()

            @pl.when(yh == 0)
            def _():
                y_copies[c, p][0].start()

            @pl.when(core == 0)
            def _():
                s_copies[A, c, p].start()

    w_copies, w_z, w_sib = {}, {}, {}

    def w_rows(slot, parity):
        return pl.ds(pl.multiple_of(slot * HALF + parity * QUARTER, QUARTER), QUARTER)

    own_rows = pl.ds(pl.multiple_of(core * HALF + zpar * QUARTER, QUARTER), QUARTER)
    for r in (1, 0):
        for slot, device, xx in ((1, x_next, (x + 1) % 4), (2, x_prev, (x + 3) % 4), (3, x_far, (x + 2) % 4)):
            w_copies[slot, r] = send(w_hbm.at[own_rows, columns(r, xx)],
                                     wts.at[core, w_rows(slot, zpar), pl.ds(r * BLK, BLK)], device)

    def weights_on(r):
        for slot in (1, 2, 3):
            w_copies[slot, r].wait_recv()
            mine = wts.at[core, w_rows(slot, zpar), pl.ds(r * BLK, BLK)]
            w_z[slot, r] = send(mine, mine, z_pair)
            w_sib[slot, r, 0] = send(mine, mine, sibling)

    def weights_share(r):
        for slot in (1, 2, 3):
            w_z[slot, r].wait_recv()
            theirs = wts.at[core, w_rows(slot, 1 - zpar), pl.ds(r * BLK, BLK)]
            w_sib[slot, r, 1] = send(theirs, theirs, sibling)

    def weights_wait(r):
        for slot in (1, 2, 3):
            for part_of in range(2):
                w_sib[slot, r, part_of].wait_recv()

    def z_arrives(c, p):
        rows = pieces[p]

        @pl.when(jnp.logical_not(first_z))
        def _():
            z_copies[c, p].wait_recv()

            @pl.when(yh == 1)
            def _():
                y_copies[c, p][1].start()

        @pl.when(core == 1)
        def _():
            remote(halo.at[Z, c, rows], halo.at[B, c, rows], s_sems[B, c, p], sibling).start()

    def y_arrives(c, p):
        rows = pieces[p]

        @pl.when(gets_y)
        def _():
            y_copies[c, p][0].wait_recv()

        @pl.when(core == 0)
        def _():
            remote(halo.at[Y, c, rows], halo.at[B, c, rows], s_sems[B, c, p], sibling).start()

        @pl.when(core == 1)
        def _():
            remote(halo.at[Y, c, rows], halo.at[A, c, rows], s_sems[A, c, p], sibling).start()

    def shared(c, slot):
        for p in range(HC):
            s_copies[slot, c, p].wait_recv()

    even_odd = [pl.ds(g * HALF, HALF) for g in range(4)]

    def filter_kernels(c, d):
        taps = filt[c, pl.ds(d * BLK, BLK), :]
        for g, rows in enumerate(even_odd):
            part_g = jnp.dot(fwd[rows], taps, preferred_element_type=F32)
            turned = -part_g if g % 2 else part_g
            kern[d, c, rows] = kern[d, c, rows] + turned if d else turned
            kern[d + 1, c, rows] = part_g

    def spectrum(c, d):
        block = halo[d, c, pl.ds(0, BLK)]
        if d:
            same = halo[d, c, pl.ds(BLK, TAG)].astype(F32)[0:1] == seg_ref[0].astype(F32)
            keep = jnp.where(jnp.logical_and(same, ctx >= d), 1.0, 0.0)
        for rows in even_odd:
            value = jnp.dot(fwd[rows], block, preferred_element_type=F32)
            spec[d, rows] = value * keep if d else value

    def product(c):
        def rows_at(start, rows, first):
            re_rows, im_rows = pl.ds(start, rows), pl.ds(start + BLK, rows)
            re, im = 0.0, 0.0
            if first:
                zeroth = lax.broadcasted_iota(jnp.int32, (rows, HALF), 0) == 0
            for d in range(REACH + 1):
                a_r, a_i = spec[d, re_rows], spec[d, im_rows]
                g_r, g_i = kern[d, c, re_rows], kern[d, c, im_rows]
                rr, ii, ri, ir = a_r * g_r, a_i * g_i, a_r * g_i, a_i * g_r
                if first:
                    re = re + (rr - jnp.where(zeroth, 0.0, ii))
                    im = im + jnp.where(zeroth, ii, ri + ir)
                else:
                    re = re + (rr - ii)
                    im = im + (ri + ir)
            acc[re_rows] = re.astype(BF16)
            acc[im_rows] = im.astype(BF16)

        @pl.loop(0, BLK // 64)
        def _(step):
            for u in range(4):
                rows_at(pl.multiple_of(step * 64 + u * 16, 16), 16, False)

        rows_at(0, 16, True)

    g_copies = {}

    def slot_lanes(slot):
        return pl.ds(slot * HALF, HALF)

    def gate(c, r):
        rows = pl.ds(r * GR, GR)
        value = jnp.dot(bwd[rows], acc[...], preferred_element_type=F32)
        gated[c, rows, slot_lanes(0)] = (q[c, rows].astype(F32) * value).astype(BF16)

    def give(c, r):
        rows = pl.ds(r * GR, GR)
        own = gated.at[c, rows, slot_lanes(0)]
        g_copies[1, c, r] = send(own, gated.at[c, rows, slot_lanes(1)], x_next)
        g_copies[2, c, r] = send(own, gated.at[c, rows, slot_lanes(2)], x_prev)

    def pass_on(c, r):
        low, high = pl.ds(r * GR, GR // 2), pl.ds(r * GR + GR // 2, GR // 2)
        for slot, rows, device in ((1, low, x_next), (2, high, x_prev)):
            g_copies[slot, c, r].wait_recv()
            g_copies[3, c, r, slot] = send(gated.at[c, rows, slot_lanes(slot)], gated.at[c, rows, slot_lanes(3)], device)

    def gathered(c, r):
        for slot in (1, 2):
            g_copies[3, c, r, slot].wait_recv()

    load_fwd.wait()
    load_filt[0].wait()
    spectrum(0, X)
    for d in range(REACH):
        filter_kernels(0, d)
    load_filt[1].wait()
    for p in range(HC):
        z_arrives(0, p)
        filter_kernels(1, p)
    load_bwd.wait()
    load_q[0].wait()
    load_q[1].wait()
    weights_on(1)
    for p in range(HC):
        y_arrives(0, p)
    spectrum(0, Z)
    z_arrives(1, 0)
    spectrum(0, Y)
    z_arrives(1, 1)
    shared(0, A)
    spectrum(0, A)
    z_arrives(1, 2)
    shared(0, B)
    spectrum(0, B)
    z_arrives(1, 3)
    product(0)
    for r in range(GC):
        gate(0, r)
        give(0, r)
    spectrum(1, X)
    spectrum(1, Z)
    weights_on(0)
    for p in range(HC):
        y_arrives(1, p)
    pass_on(0, 0)
    pass_on(0, 1)
    spectrum(1, Y)
    shared(1, A)
    spectrum(1, A)
    shared(1, B)
    spectrum(1, B)
    product(1)
    gate(1, 0)
    give(1, 0)
    pass_on(0, 2)
    gate(1, 1)
    give(1, 1)
    pass_on(0, 3)
    gate(1, 2)
    gate(1, 3)

    own_cols, other_cols = pl.ds(0, BLK), pl.ds(BLK, BLK)

    def project(c, rows, cols):
        return jnp.dot(gated[c, rows], wts[c, :, cols], preferred_element_type=F32)

    everything = pl.ds(0, BLK)
    swaps = []

    def swap(r):
        rows = pl.ds(r * GR, GR)
        gathered(1, r)
        ysend[rows] = (part[rows, other_cols] + project(1, rows, other_cols)).astype(BF16)
        swaps.append(send(ysend.at[rows], yrecv.at[rows], y_pair))

    weights_share(1)
    for copy in load_w:
        copy.wait()
    pass_on(1, 0)
    give(1, 2)
    pass_on(1, 1)
    give(1, 3)
    for r in range(GC):
        gathered(0, r)
    weights_wait(1)
    part[:, other_cols] = project(0, everything, other_cols)
    swap(0)
    pass_on(1, 2)
    swap(1)
    pass_on(1, 3)
    swap(2)
    swap(3)
    weights_share(0)
    weights_wait(0)
    part[:, own_cols] = project(0, everything, own_cols) + project(1, everything, own_cols)
    for r in range(GC):
        rows = pl.ds(r * GR, GR)
        swaps[r].wait_recv()
        out_ref[rows] = (part[rows, own_cols] + yrecv[rows].astype(F32)).astype(BF16)
    for copy in always:
        copy.wait_send()
    for condition, copy in by_condition:
        @pl.when(condition)
        def _():
            copy.wait_send()


def on_device(query, keys, values, filters, segment_ids, out_weight):
    forward, backward = tables()
    anywhere = pl.BlockSpec(memory_space=pl.ANY)
    return pl.pallas_call(
        kernel,
        out_shape=jax.ShapeDtypeStruct((BLK, BLK), BF16),
        in_specs=[pl.BlockSpec(memory_space=pltpu.SMEM)] + [anywhere] * 7,
        out_specs=pl.BlockSpec(memory_space=pltpu.VMEM),
        scratch_shapes=[
            pltpu.VMEM((NC, BLK, HALF), BF16),
            pltpu.VMEM((NC, BLK, HALF), BF16),
            pltpu.VMEM((NC, BLK, HALF), BF16),
            pltpu.VMEM((NC, REACH * BLK, HALF), BF16),
            pltpu.VMEM((2 * BLK, BLK), BF16),
            pltpu.VMEM((BLK, 2 * BLK), BF16),
            pltpu.VMEM((REACH + 1, NC, ROWS, HALF), BF16),
            pltpu.VMEM((REACH + 1, NC, 2 * BLK, HALF), F32),
            pltpu.VMEM((REACH + 1, 2 * BLK, HALF), F32),
            pltpu.VMEM((2 * BLK, HALF), BF16),
            pltpu.VMEM((NC, BLK, 4 * HALF), BF16),
            pltpu.VMEM((NC, 4 * HALF, 2 * BLK), BF16),
            pltpu.VMEM((BLK, 2 * BLK), F32),
            pltpu.VMEM((BLK, BLK), BF16),
            pltpu.VMEM((BLK, BLK), BF16),
            pltpu.SemaphoreType.DMA((16,)),
            pltpu.SemaphoreType.DMA((96,)),
            pltpu.SemaphoreType.DMA((96,)),
        ],
        compiler_params=pltpu.CompilerParams(collective_id=0, has_side_effects=True, vmem_limit_bytes=56 * 2**20),
        name="hyena",
    )(segment_ids, query, keys, values, filters, out_weight, jnp.asarray(forward), jnp.asarray(backward))


def solution(mesh):
    in_specs = (
        P("ctx", "ch"),
        P("ctx", "ch"),
        P("ctx", "ch"),
        P(None, "ch"),
        P("ctx"),
        P("ch", None),
    )
    return jax.shard_map(on_device, mesh=mesh, in_specs=in_specs, out_specs=P("ctx", "ch"), check_vma=False)
```

```python
import functools
import math

import jax
import jax.numpy as jnp
import ml_dtypes
import numpy as np
from jax import lax
from jax.experimental import pallas as pl
from jax.experimental.pallas import tpu as pltpu
from jax.sharding import PartitionSpec as P

MESH = pl.DeviceIdType.MESH
BF16, F32 = jnp.bfloat16, jnp.float32

BLK = 512
HALF = 256
NC = BLK // HALF
TAG = 16
ROWS = BLK + TAG
HALO_CUTS = (0, 160, 320, 448, ROWS)
HC = len(HALO_CUTS) - 1
GC = 4
GR = BLK // GC
QUARTER = BLK // 4
REACH = 4


def tables():
    period = 2 * BLK
    order = np.concatenate([np.arange(0, BLK, 2), np.arange(1, BLK, 2)])

    def angle(freq, pos):
        return (np.float32(2.0 * math.pi / period) * ((freq * pos) % period).astype(np.float32)).astype(np.float32)

    forward_angles = angle(order[:, None], np.arange(BLK)[None, :])
    real, imag = np.cos(forward_angles), -np.sin(forward_angles)
    imag[0] = np.cos(angle(np.full((1, 1), BLK), np.arange(BLK)[None, :]))[0]
    forward = np.concatenate([real, imag], 0).astype(ml_dtypes.bfloat16)
    out_rows = np.arange(BLK)[:, None] + BLK
    back_angles = angle(out_rows, order[None, :])
    real, imag = 2 * np.cos(back_angles), -2 * np.sin(back_angles)
    real[:, 0] = 1.0
    imag[:, 0] = np.cos(angle(out_rows, np.full((1, 1), BLK)))[:, 0]
    backward = (np.concatenate([real, imag], 1) / np.float32(period)).astype(ml_dtypes.bfloat16)
    return forward, backward


def kernel(seg_ref, q_hbm, k_hbm, v_hbm, filt_hbm, w_hbm, fwd_hbm, bwd_hbm, out_ref,
           q, k, v, filt, fwd, bwd, halo, kern, spec, acc, gated, wts, part, ysend, yrecv, lsem, ssem, rsem):
    ctx, ch = lax.axis_index("ctx"), lax.axis_index("ch")
    z, yh, core = ctx // 4, (ctx // 2) % 2, ctx % 2
    yl, x = ch // 4, ch % 4
    zpar = z % 2
    sibling = (z * 4 + yh * 2 + 1 - core, ch)
    y_pair = (ctx, (1 - yl) * 4 + x)
    y_far = (z * 4 + (1 - yh) * 2 + core, ch)
    z_next, z_prev = (((z + 1) % 8) * 4 + yh * 2 + core, ch), (((z + 7) % 8) * 4 + yh * 2 + core, ch)
    z_pair = ((z + 1 - 2 * zpar) * 4 + yh * 2 + core, ch)
    x_next, x_prev = (ctx, yl * 4 + (x + 1) % 4), (ctx, yl * 4 + (x + 3) % 4)
    x_far = (ctx, yl * 4 + (x + 2) % 4)
    first_z, last_z = z == 0, z == 7

    def signal(device):
        pl.semaphore_signal(barrier, inc=1, device_id=device, device_id_type=MESH)

    barrier = pltpu.get_barrier_semaphore()
    for device in (sibling, y_pair, y_far, x_next, x_prev, x_far):
        signal(device)

    @pl.when(jnp.logical_not(first_z))
    def _():
        signal(z_prev)

    @pl.when(jnp.logical_not(last_z))
    def _():
        signal(z_next)

    counter = [0, 0]
    always, by_condition = [], []

    def number():
        counter[0] += 1
        return counter[0] - 1

    def remote(src, dst, sem, device):
        return pltpu.make_async_remote_copy(src_ref=src, dst_ref=dst, send_sem=ssem.at[sem], recv_sem=rsem.at[sem],
                                            device_id=device, device_id_type=MESH)

    def send(src, dst, device):
        copy = remote(src, dst, number(), device)
        copy.start()
        always.append(copy)
        return copy

    def load(src, dst):
        copy = pltpu.make_async_copy(src, dst, lsem.at[counter[1]])
        counter[1] += 1
        copy.start()
        return copy

    X, A, Y, B, Z = 0, 1, 2, 3, 4
    lanes = [pl.ds(c * HALF, HALF) for c in range(NC)]
    kv = [(load(k_hbm.at[:, lanes[c]], k.at[c]), load(v_hbm.at[:, lanes[c]], v.at[c])) for c in range(NC)]
    load_fwd = load(fwd_hbm, fwd)
    load_filt = [load(filt_hbm.at[:, lanes[c]], filt.at[c]) for c in range(NC)]
    load_bwd = load(bwd_hbm, bwd)
    load_q = [load(q_hbm.at[:, lanes[c]], q.at[c]) for c in range(NC)]

    def columns(r, xx):
        yy = yl if r == 0 else 1 - yl
        return pl.ds(pl.multiple_of((yy * 4 + xx) * BLK, BLK), BLK)

    load_w = [load(w_hbm.at[pl.ds(c * HALF, HALF), columns(r, x)], wts.at[c, pl.ds(0, HALF), pl.ds(r * BLK, BLK)])
              for c in range(NC) for r in range(2)]

    @pl.when(first_z)
    def _():
        halo[Z] = jnp.zeros((NC, ROWS, HALF), BF16)

        @pl.when(yh == 0)
        def _():
            halo[Y] = jnp.zeros((NC, ROWS, HALF), BF16)

    tag = jnp.full((TAG, HALF), seg_ref[0].astype(F32)).astype(BF16)

    def mix(c):
        for copy in kv[c]:
            copy.wait()
        halo[X, c, pl.ds(0, BLK)] = (k[c].astype(F32) * v[c].astype(F32)).astype(BF16)
        halo[X, c, pl.ds(BLK, TAG)] = tag

    mix(0)
    pl.semaphore_wait(barrier, 8 - first_z.astype(jnp.int32) - last_z.astype(jnp.int32))

    pieces = [pl.ds(HALO_CUTS[p], HALO_CUTS[p + 1] - HALO_CUTS[p]) for p in range(HC)]
    z_copies, y_copies, s_copies, s_sems = {}, {}, {}, {}
    gets_y = jnp.logical_or(yh == 1, jnp.logical_not(first_z))
    gives_y = jnp.logical_or(yh == 0, jnp.logical_not(first_z))
    for c in range(NC):
        if c:
            mix(c)
        for p, rows in enumerate(pieces):
            z_copies[c, p] = remote(halo.at[X, c, rows], halo.at[Z, c, rows], number(), z_next)
            y_copies[c, p] = [remote(halo.at[src, c, rows], halo.at[Y, c, rows], counter[0], y_far) for src in (X, Z)]
            number()
            s_sems[A, c, p], s_sems[B, c, p] = number(), number()
            by_condition.append((jnp.logical_not(last_z), z_copies[c, p]))
            by_condition.append((gives_y, y_copies[c, p][0]))
            for slot in (A, B):
                s_copies[slot, c, p] = remote(halo.at[X, c, rows], halo.at[slot, c, rows], s_sems[slot, c, p], sibling)
                always.append(s_copies[slot, c, p])

            @pl.when(jnp.logical_not(last_z))
            def _():
                z_copies[c, p].start()

            @pl.when(yh == 0)
            def _():
                y_copies[c, p][0].start()

            @pl.when(core == 0)
            def _():
                s_copies[A, c, p].start()

    w_copies, w_z, w_sib = {}, {}, {}

    def w_rows(slot, parity):
        return pl.ds(pl.multiple_of(slot * HALF + parity * QUARTER, QUARTER), QUARTER)

    own_rows = pl.ds(pl.multiple_of(core * HALF + zpar * QUARTER, QUARTER), QUARTER)
    for r in (1, 0):
        for slot, device, xx in ((1, x_next, (x + 1) % 4), (2, x_prev, (x + 3) % 4), (3, x_far, (x + 2) % 4)):
            w_copies[slot, r] = send(w_hbm.at[own_rows, columns(r, xx)],
                                     wts.at[core, w_rows(slot, zpar), pl.ds(r * BLK, BLK)], device)

    def weights_on(r):
        for slot in (1, 2, 3):
            w_copies[slot, r].wait_recv()
            mine = wts.at[core, w_rows(slot, zpar), pl.ds(r * BLK, BLK)]
            w_z[slot, r] = send(mine, mine, z_pair)
            w_sib[slot, r, 0] = send(mine, mine, sibling)

    def weights_share(r):
        for slot in (1, 2, 3):
            w_z[slot, r].wait_recv()
            theirs = wts.at[core, w_rows(slot, 1 - zpar), pl.ds(r * BLK, BLK)]
            w_sib[slot, r, 1] = send(theirs, theirs, sibling)

    def weights_wait(r):
        for slot in (1, 2, 3):
            for part_of in range(2):
                w_sib[slot, r, part_of].wait_recv()

    def z_arrives(c, p):
        rows = pieces[p]

        @pl.when(jnp.logical_not(first_z))
        def _():
            z_copies[c, p].wait_recv()

            @pl.when(yh == 1)
            def _():
                y_copies[c, p][1].start()

        @pl.when(core == 1)
        def _():
            remote(halo.at[Z, c, rows], halo.at[B, c, rows], s_sems[B, c, p], sibling).start()

    def y_arrives(c, p):
        rows = pieces[p]

        @pl.when(gets_y)
        def _():
            y_copies[c, p][0].wait_recv()

        @pl.when(core == 0)
        def _():
            remote(halo.at[Y, c, rows], halo.at[B, c, rows], s_sems[B, c, p], sibling).start()

        @pl.when(core == 1)
        def _():
            remote(halo.at[Y, c, rows], halo.at[A, c, rows], s_sems[A, c, p], sibling).start()

    def shared(c, slot):
        for p in range(HC):
            s_copies[slot, c, p].wait_recv()

    even_odd = [pl.ds(g * HALF, HALF) for g in range(4)]

    def filter_kernels(c, d):
        taps = filt[c, pl.ds(d * BLK, BLK), :]
        for g, rows in enumerate(even_odd):
            part_g = jnp.dot(fwd[rows], taps, preferred_element_type=F32)
            turned = -part_g if g % 2 else part_g
            kern[d, c, rows] = kern[d, c, rows] + turned if d else turned
            kern[d + 1, c, rows] = part_g

    def spectrum(c, d):
        block = halo[d, c, pl.ds(0, BLK)]
        if d:
            same = halo[d, c, pl.ds(BLK, TAG)].astype(F32)[0:1] == seg_ref[0].astype(F32)
            keep = jnp.where(jnp.logical_and(same, ctx >= d), 1.0, 0.0)
        for rows in even_odd:
            value = jnp.dot(fwd[rows], block, preferred_element_type=F32)
            spec[d, rows] = value * keep if d else value

    def product(c):
        def rows_at(start, rows, first):
            re_rows, im_rows = pl.ds(start, rows), pl.ds(start + BLK, rows)
            re, im = 0.0, 0.0
            if first:
                zeroth = lax.broadcasted_iota(jnp.int32, (rows, HALF), 0) == 0
            for d in range(REACH + 1):
                a_r, a_i = spec[d, re_rows], spec[d, im_rows]
                g_r, g_i = kern[d, c, re_rows], kern[d, c, im_rows]
                rr, ii, ri, ir = a_r * g_r, a_i * g_i, a_r * g_i, a_i * g_r
                if first:
                    re = re + (rr - jnp.where(zeroth, 0.0, ii))
                    im = im + jnp.where(zeroth, ii, ri + ir)
                else:
                    re = re + (rr - ii)
                    im = im + (ri + ir)
            acc[re_rows] = re.astype(BF16)
            acc[im_rows] = im.astype(BF16)

        @pl.loop(0, BLK // 64)
        def _(step):
            for u in range(4):
                rows_at(pl.multiple_of(step * 64 + u * 16, 16), 16, False)

        rows_at(0, 16, True)

    g_copies = {}

    def slot_lanes(slot):
        return pl.ds(slot * HALF, HALF)

    def gate(c, r):
        rows = pl.ds(r * GR, GR)
        value = jnp.dot(bwd[rows], acc[...], preferred_element_type=F32)
        gated[c, rows, slot_lanes(0)] = (q[c, rows].astype(F32) * value).astype(BF16)

    def give(c, r):
        rows = pl.ds(r * GR, GR)
        own = gated.at[c, rows, slot_lanes(0)]
        g_copies[1, c, r] = send(own, gated.at[c, rows, slot_lanes(1)], x_next)
        g_copies[2, c, r] = send(own, gated.at[c, rows, slot_lanes(2)], x_prev)

    def pass_on(c, r):
        low, high = pl.ds(r * GR, GR // 2), pl.ds(r * GR + GR // 2, GR // 2)
        for slot, rows, device in ((1, low, x_next), (2, high, x_prev)):
            g_copies[slot, c, r].wait_recv()
            g_copies[3, c, r, slot] = send(gated.at[c, rows, slot_lanes(slot)], gated.at[c, rows, slot_lanes(3)], device)

    def gathered(c, r):
        for slot in (1, 2):
            g_copies[3, c, r, slot].wait_recv()

    load_fwd.wait()
    load_filt[0].wait()
    spectrum(0, X)
    for d in range(REACH):
        filter_kernels(0, d)
    load_filt[1].wait()
    for p in range(HC):
        z_arrives(0, p)
        filter_kernels(1, p)
    load_bwd.wait()
    load_q[0].wait()
    load_q[1].wait()
    weights_on(1)
    for p in range(HC):
        y_arrives(0, p)
    spectrum(0, Z)
    z_arrives(1, 0)
    spectrum(0, Y)
    z_arrives(1, 1)
    shared(0, A)
    spectrum(0, A)
    z_arrives(1, 2)
    shared(0, B)
    spectrum(0, B)
    z_arrives(1, 3)
    product(0)
    for r in range(GC):
        gate(0, r)
        give(0, r)
    spectrum(1, X)
    spectrum(1, Z)
    for p in range(HC):
        y_arrives(1, p)
    pass_on(0, 0)
    pass_on(0, 1)
    spectrum(1, Y)
    shared(1, A)
    spectrum(1, A)
    shared(1, B)
    spectrum(1, B)
    product(1)
    gate(1, 0)
    give(1, 0)
    pass_on(0, 2)
    gate(1, 1)
    give(1, 1)
    pass_on(0, 3)
    gate(1, 2)
    gate(1, 3)
    weights_on(0)

    own_cols, other_cols = pl.ds(0, BLK), pl.ds(BLK, BLK)

    def project(c, rows, cols):
        return jnp.dot(gated[c, rows], wts[c, :, cols], preferred_element_type=F32)

    everything = pl.ds(0, BLK)
    swaps = []

    def swap(r):
        rows = pl.ds(r * GR, GR)
        gathered(1, r)
        ysend[rows] = (part[rows, other_cols] + project(1, rows, other_cols)).astype(BF16)
        swaps.append(send(ysend.at[rows], yrecv.at[rows], y_pair))

    weights_share(1)
    for copy in load_w:
        copy.wait()
    pass_on(1, 0)
    give(1, 2)
    pass_on(1, 1)
    give(1, 3)
    for r in range(GC):
        gathered(0, r)
    weights_wait(1)
    part[:, other_cols] = project(0, everything, other_cols)
    swap(0)
    pass_on(1, 2)
    swap(1)
    pass_on(1, 3)
    swap(2)
    swap(3)
    weights_share(0)
    weights_wait(0)
    part[:, own_cols] = project(0, everything, own_cols) + project(1, everything, own_cols)
    for r in range(GC):
        rows = pl.ds(r * GR, GR)
        swaps[r].wait_recv()
        out_ref[rows] = (part[rows, own_cols] + yrecv[rows].astype(F32)).astype(BF16)
    for copy in always:
        copy.wait_send()
    for condition, copy in by_condition:
        @pl.when(condition)
        def _():
            copy.wait_send()


def on_device(query, keys, values, filters, segment_ids, out_weight):
    forward, backward = tables()
    anywhere = pl.BlockSpec(memory_space=pl.ANY)
    return pl.pallas_call(
        kernel,
        out_shape=jax.ShapeDtypeStruct((BLK, BLK), BF16),
        in_specs=[pl.BlockSpec(memory_space=pltpu.SMEM)] + [anywhere] * 7,
        out_specs=pl.BlockSpec(memory_space=pltpu.VMEM),
        scratch_shapes=[
            pltpu.VMEM((NC, BLK, HALF), BF16),
            pltpu.VMEM((NC, BLK, HALF), BF16),
            pltpu.VMEM((NC, BLK, HALF), BF16),
            pltpu.VMEM((NC, REACH * BLK, HALF), BF16),
            pltpu.VMEM((2 * BLK, BLK), BF16),
            pltpu.VMEM((BLK, 2 * BLK), BF16),
            pltpu.VMEM((REACH + 1, NC, ROWS, HALF), BF16),
            pltpu.VMEM((REACH + 1, NC, 2 * BLK, HALF), F32),
            pltpu.VMEM((REACH + 1, 2 * BLK, HALF), F32),
            pltpu.VMEM((2 * BLK, HALF), BF16),
            pltpu.VMEM((NC, BLK, 4 * HALF), BF16),
            pltpu.VMEM((NC, 4 * HALF, 2 * BLK), BF16),
            pltpu.VMEM((BLK, 2 * BLK), F32),
            pltpu.VMEM((BLK, BLK), BF16),
            pltpu.VMEM((BLK, BLK), BF16),
            pltpu.SemaphoreType.DMA((16,)),
            pltpu.SemaphoreType.DMA((96,)),
            pltpu.SemaphoreType.DMA((96,)),
        ],
        compiler_params=pltpu.CompilerParams(collective_id=0, has_side_effects=True, vmem_limit_bytes=56 * 2**20),
        name="hyena",
    )(segment_ids, query, keys, values, filters, out_weight, jnp.asarray(forward), jnp.asarray(backward))


def solution(mesh):
    in_specs = (
        P("ctx", "ch"),
        P("ctx", "ch"),
        P("ctx", "ch"),
        P(None, "ch"),
        P("ctx"),
        P("ch", None),
    )
    return jax.shard_map(on_device, mesh=mesh, in_specs=in_specs, out_specs=P("ctx", "ch"), check_vma=False)
```

```python
import functools
import math

import jax
import jax.numpy as jnp
import ml_dtypes
import numpy as np
from jax import lax
from jax.experimental import pallas as pl
from jax.experimental.pallas import tpu as pltpu
from jax.sharding import PartitionSpec as P

MESH = pl.DeviceIdType.MESH
BF16, F32 = jnp.bfloat16, jnp.float32

BLK = 512
HALF = 256
NC = BLK // HALF
TAG = 16
ROWS = BLK + TAG
HALO_CUTS = (0, 176, 336, 464, ROWS)
HC = len(HALO_CUTS) - 1
GC = 4
GR = BLK // GC
QUARTER = BLK // 4
REACH = 4


def tables():
    period = 2 * BLK
    order = np.concatenate([np.arange(0, BLK, 2), np.arange(1, BLK, 2)])

    def angle(freq, pos):
        return (np.float32(2.0 * math.pi / period) * ((freq * pos) % period).astype(np.float32)).astype(np.float32)

    forward_angles = angle(order[:, None], np.arange(BLK)[None, :])
    real, imag = np.cos(forward_angles), -np.sin(forward_angles)
    imag[0] = np.cos(angle(np.full((1, 1), BLK), np.arange(BLK)[None, :]))[0]
    forward = np.concatenate([real, imag], 0).astype(ml_dtypes.bfloat16)
    out_rows = np.arange(BLK)[:, None] + BLK
    back_angles = angle(out_rows, order[None, :])
    real, imag = 2 * np.cos(back_angles), -2 * np.sin(back_angles)
    real[:, 0] = 1.0
    imag[:, 0] = np.cos(angle(out_rows, np.full((1, 1), BLK)))[:, 0]
    backward = (np.concatenate([real, imag], 1) / np.float32(period)).astype(ml_dtypes.bfloat16)
    return forward, backward


def kernel(seg_ref, q_hbm, k_hbm, v_hbm, filt_hbm, w_hbm, fwd_hbm, bwd_hbm, out_ref,
           q, k, v, filt, fwd, bwd, halo, kern, spec, acc, gated, wts, part, ysend, yrecv, lsem, ssem, rsem):
    ctx, ch = lax.axis_index("ctx"), lax.axis_index("ch")
    z, yh, core = ctx // 4, (ctx // 2) % 2, ctx % 2
    yl, x = ch // 4, ch % 4
    zpar = z % 2
    sibling = (z * 4 + yh * 2 + 1 - core, ch)
    y_pair = (ctx, (1 - yl) * 4 + x)
    y_far = (z * 4 + (1 - yh) * 2 + core, ch)
    z_next, z_prev = (((z + 1) % 8) * 4 + yh * 2 + core, ch), (((z + 7) % 8) * 4 + yh * 2 + core, ch)
    z_pair = ((z + 1 - 2 * zpar) * 4 + yh * 2 + core, ch)
    x_next, x_prev = (ctx, yl * 4 + (x + 1) % 4), (ctx, yl * 4 + (x + 3) % 4)
    x_far = (ctx, yl * 4 + (x + 2) % 4)
    first_z, last_z = z == 0, z == 7

    def signal(device):
        pl.semaphore_signal(barrier, inc=1, device_id=device, device_id_type=MESH)

    barrier = pltpu.get_barrier_semaphore()
    for device in (sibling, y_pair, y_far, x_next, x_prev, x_far):
        signal(device)

    @pl.when(jnp.logical_not(first_z))
    def _():
        signal(z_prev)

    @pl.when(jnp.logical_not(last_z))
    def _():
        signal(z_next)

    counter = [0, 0]
    always, by_condition = [], []

    def number():
        counter[0] += 1
        return counter[0] - 1

    def remote(src, dst, sem, device):
        return pltpu.make_async_remote_copy(src_ref=src, dst_ref=dst, send_sem=ssem.at[sem], recv_sem=rsem.at[sem],
                                            device_id=device, device_id_type=MESH)

    def send(src, dst, device):
        copy = remote(src, dst, number(), device)
        copy.start()
        always.append(copy)
        return copy

    def load(src, dst):
        copy = pltpu.make_async_copy(src, dst, lsem.at[counter[1]])
        counter[1] += 1
        copy.start()
        return copy

    X, A, Y, B, Z = 0, 1, 2, 3, 4
    lanes = [pl.ds(c * HALF, HALF) for c in range(NC)]
    kv = [(load(k_hbm.at[:, lanes[c]], k.at[c]), load(v_hbm.at[:, lanes[c]], v.at[c])) for c in range(NC)]
    load_fwd = load(fwd_hbm, fwd)
    load_filt = [load(filt_hbm.at[:, lanes[c]], filt.at[c]) for c in range(NC)]
    load_bwd = load(bwd_hbm, bwd)
    load_q = [load(q_hbm.at[:, lanes[c]], q.at[c]) for c in range(NC)]

    def columns(r, xx):
        yy = yl if r == 0 else 1 - yl
        return pl.ds(pl.multiple_of((yy * 4 + xx) * BLK, BLK), BLK)

    load_w = [load(w_hbm.at[pl.ds(c * HALF, HALF), columns(r, x)], wts.at[c, pl.ds(0, HALF), pl.ds(r * BLK, BLK)])
              for c in range(NC) for r in range(2)]

    @pl.when(first_z)
    def _():
        halo[Z] = jnp.zeros((NC, ROWS, HALF), BF16)

        @pl.when(yh == 0)
        def _():
            halo[Y] = jnp.zeros((NC, ROWS, HALF), BF16)

    tag = jnp.full((TAG, HALF), seg_ref[0].astype(F32)).astype(BF16)

    def mix(c):
        for copy in kv[c]:
            copy.wait()
        halo[X, c, pl.ds(0, BLK)] = (k[c].astype(F32) * v[c].astype(F32)).astype(BF16)
        halo[X, c, pl.ds(BLK, TAG)] = tag

    mix(0)
    pl.semaphore_wait(barrier, 8 - first_z.astype(jnp.int32) - last_z.astype(jnp.int32))

    pieces = [pl.ds(HALO_CUTS[p], HALO_CUTS[p + 1] - HALO_CUTS[p]) for p in range(HC)]
    z_copies, y_copies, s_copies, s_sems = {}, {}, {}, {}
    gets_y = jnp.logical_or(yh == 1, jnp.logical_not(first_z))
    gives_y = jnp.logical_or(yh == 0, jnp.logical_not(first_z))
    for c in range(NC):
        if c:
            mix(c)
        for p, rows in enumerate(pieces):
            z_copies[c, p] = remote(halo.at[X, c, rows], halo.at[Z, c, rows], number(), z_next)
            y_copies[c, p] = [remote(halo.at[src, c, rows], halo.at[Y, c, rows], counter[0], y_far) for src in (X, Z)]
            number()
            s_sems[A, c, p], s_sems[B, c, p] = number(), number()
            by_condition.append((jnp.logical_not(last_z), z_copies[c, p]))
            by_condition.append((gives_y, y_copies[c, p][0]))
            for slot in (A, B):
                s_copies[slot, c, p] = remote(halo.at[X, c, rows], halo.at[slot, c, rows], s_sems[slot, c, p], sibling)
                always.append(s_copies[slot, c, p])

            @pl.when(jnp.logical_not(last_z))
            def _():
                z_copies[c, p].start()

            @pl.when(yh == 0)
            def _():
                y_copies[c, p][0].start()

            @pl.when(core == 0)
            def _():
                s_copies[A, c, p].start()

    w_copies, w_z, w_sib = {}, {}, {}

    def w_rows(slot, parity):
        return pl.ds(pl.multiple_of(slot * HALF + parity * QUARTER, QUARTER), QUARTER)

    own_rows = pl.ds(pl.multiple_of(core * HALF + zpar * QUARTER, QUARTER), QUARTER)
    for r in (1, 0):
        for slot, device, xx in ((1, x_next, (x + 1) % 4), (2, x_prev, (x + 3) % 4), (3, x_far, (x + 2) % 4)):
            w_copies[slot, r] = send(w_hbm.at[own_rows, columns(r, xx)],
                                     wts.at[core, w_rows(slot, zpar), pl.ds(r * BLK, BLK)], device)

    def weights_on(r):
        for slot in (1, 2, 3):
            w_copies[slot, r].wait_recv()
            mine = wts.at[core, w_rows(slot, zpar), pl.ds(r * BLK, BLK)]
            w_z[slot, r] = send(mine, mine, z_pair)
            w_sib[slot, r, 0] = send(mine, mine, sibling)

    def weights_share(r):
        for slot in (1, 2, 3):
            w_z[slot, r].wait_recv()
            theirs = wts.at[core, w_rows(slot, 1 - zpar), pl.ds(r * BLK, BLK)]
            w_sib[slot, r, 1] = send(theirs, theirs, sibling)

    def weights_wait(r):
        for slot in (1, 2, 3):
            for part_of in range(2):
                w_sib[slot, r, part_of].wait_recv()

    def z_arrives(c, p):
        rows = pieces[p]

        @pl.when(jnp.logical_not(first_z))
        def _():
            z_copies[c, p].wait_recv()

            @pl.when(yh == 1)
            def _():
                y_copies[c, p][1].start()

        @pl.when(core == 1)
        def _():
            remote(halo.at[Z, c, rows], halo.at[B, c, rows], s_sems[B, c, p], sibling).start()

    def y_arrives(c, p):
        rows = pieces[p]

        @pl.when(gets_y)
        def _():
            y_copies[c, p][0].wait_recv()

        @pl.when(core == 0)
        def _():
            remote(halo.at[Y, c, rows], halo.at[B, c, rows], s_sems[B, c, p], sibling).start()

        @pl.when(core == 1)
        def _():
            remote(halo.at[Y, c, rows], halo.at[A, c, rows], s_sems[A, c, p], sibling).start()

    def shared(c, slot):
        for p in range(HC):
            s_copies[slot, c, p].wait_recv()

    even_odd = [pl.ds(g * HALF, HALF) for g in range(4)]

    def filter_kernels(c, d):
        taps = filt[c, pl.ds(d * BLK, BLK), :]
        for g, rows in enumerate(even_odd):
            part_g = jnp.dot(fwd[rows], taps, preferred_element_type=F32)
            turned = -part_g if g % 2 else part_g
            kern[d, c, rows] = kern[d, c, rows] + turned if d else turned
            kern[d + 1, c, rows] = part_g

    def spectrum(c, d):
        block = halo[d, c, pl.ds(0, BLK)]
        if d:
            same = halo[d, c, pl.ds(BLK, TAG)].astype(F32)[0:1] == seg_ref[0].astype(F32)
            keep = jnp.where(jnp.logical_and(same, ctx >= d), 1.0, 0.0)
        for rows in even_odd:
            value = jnp.dot(fwd[rows], block, preferred_element_type=F32)
            spec[d, rows] = value * keep if d else value

    def product(c):
        def rows_at(start, rows, first):
            re_rows, im_rows = pl.ds(start, rows), pl.ds(start + BLK, rows)
            re, im = 0.0, 0.0
            if first:
                zeroth = lax.broadcasted_iota(jnp.int32, (rows, HALF), 0) == 0
            for d in range(REACH + 1):
                a_r, a_i = spec[d, re_rows], spec[d, im_rows]
                g_r, g_i = kern[d, c, re_rows], kern[d, c, im_rows]
                rr, ii, ri, ir = a_r * g_r, a_i * g_i, a_r * g_i, a_i * g_r
                if first:
                    re = re + (rr - jnp.where(zeroth, 0.0, ii))
                    im = im + jnp.where(zeroth, ii, ri + ir)
                else:
                    re = re + (rr - ii)
                    im = im + (ri + ir)
            acc[re_rows] = re.astype(BF16)
            acc[im_rows] = im.astype(BF16)

        @pl.loop(0, BLK // 64)
        def _(step):
            for u in range(4):
                rows_at(pl.multiple_of(step * 64 + u * 16, 16), 16, False)

        rows_at(0, 16, True)

    g_copies = {}

    def slot_lanes(slot):
        return pl.ds(slot * HALF, HALF)

    def gate(c, r):
        rows = pl.ds(r * GR, GR)
        value = jnp.dot(bwd[rows], acc[...], preferred_element_type=F32)
        gated[c, rows, slot_lanes(0)] = (q[c, rows].astype(F32) * value).astype(BF16)

    def give(c, r):
        rows = pl.ds(r * GR, GR)
        own = gated.at[c, rows, slot_lanes(0)]
        g_copies[1, c, r] = send(own, gated.at[c, rows, slot_lanes(1)], x_next)
        g_copies[2, c, r] = send(own, gated.at[c, rows, slot_lanes(2)], x_prev)

    def pass_on(c, r):
        low, high = pl.ds(r * GR, GR // 2), pl.ds(r * GR + GR // 2, GR // 2)
        for slot, rows, device in ((1, low, x_next), (2, high, x_prev)):
            g_copies[slot, c, r].wait_recv()
            g_copies[3, c, r, slot] = send(gated.at[c, rows, slot_lanes(slot)], gated.at[c, rows, slot_lanes(3)], device)

    def gathered(c, r):
        for slot in (1, 2):
            g_copies[3, c, r, slot].wait_recv()

    load_fwd.wait()
    load_filt[0].wait()
    spectrum(0, X)
    for d in range(REACH):
        filter_kernels(0, d)
    load_filt[1].wait()
    for p in range(HC):
        z_arrives(0, p)
        filter_kernels(1, p)
    load_bwd.wait()
    load_q[0].wait()
    load_q[1].wait()
    weights_on(1)
    for p in range(HC):
        y_arrives(0, p)
    spectrum(0, Z)
    z_arrives(1, 0)
    spectrum(0, Y)
    z_arrives(1, 1)
    shared(0, A)
    spectrum(0, A)
    z_arrives(1, 2)
    shared(0, B)
    spectrum(0, B)
    z_arrives(1, 3)
    product(0)
    for r in range(GC):
        gate(0, r)
        give(0, r)
    spectrum(1, X)
    spectrum(1, Z)
    for p in range(HC):
        y_arrives(1, p)
    pass_on(0, 0)
    pass_on(0, 1)
    spectrum(1, Y)
    shared(1, A)
    spectrum(1, A)
    shared(1, B)
    spectrum(1, B)
    product(1)
    gate(1, 0)
    give(1, 0)
    pass_on(0, 2)
    gate(1, 1)
    give(1, 1)
    pass_on(0, 3)
    gate(1, 2)
    gate(1, 3)
    weights_on(0)

    own_cols, other_cols = pl.ds(0, BLK), pl.ds(BLK, BLK)

    def project(c, rows, cols):
        return jnp.dot(gated[c, rows], wts[c, :, cols], preferred_element_type=F32)

    everything = pl.ds(0, BLK)
    swaps = []

    def swap(r):
        rows = pl.ds(r * GR, GR)
        gathered(1, r)
        ysend[rows] = (part[rows, other_cols] + project(1, rows, other_cols)).astype(BF16)
        swaps.append(send(ysend.at[rows], yrecv.at[rows], y_pair))

    weights_share(1)
    for copy in load_w:
        copy.wait()
    pass_on(1, 0)
    give(1, 2)
    pass_on(1, 1)
    give(1, 3)
    for r in range(GC):
        gathered(0, r)
    weights_wait(1)
    part[:, other_cols] = project(0, everything, other_cols)
    swap(0)
    pass_on(1, 2)
    swap(1)
    pass_on(1, 3)
    swap(2)
    swap(3)
    weights_share(0)
    weights_wait(0)
    part[:, own_cols] = project(0, everything, own_cols) + project(1, everything, own_cols)
    for r in range(GC):
        rows = pl.ds(r * GR, GR)
        swaps[r].wait_recv()
        out_ref[rows] = (part[rows, own_cols] + yrecv[rows].astype(F32)).astype(BF16)
    for copy in always:
        copy.wait_send()
    for condition, copy in by_condition:
        @pl.when(condition)
        def _():
            copy.wait_send()


def on_device(query, keys, values, filters, segment_ids, out_weight):
    forward, backward = tables()
    anywhere = pl.BlockSpec(memory_space=pl.ANY)
    return pl.pallas_call(
        kernel,
        out_shape=jax.ShapeDtypeStruct((BLK, BLK), BF16),
        in_specs=[pl.BlockSpec(memory_space=pltpu.SMEM)] + [anywhere] * 7,
        out_specs=pl.BlockSpec(memory_space=pltpu.VMEM),
        scratch_shapes=[
            pltpu.VMEM((NC, BLK, HALF), BF16),
            pltpu.VMEM((NC, BLK, HALF), BF16),
            pltpu.VMEM((NC, BLK, HALF), BF16),
            pltpu.VMEM((NC, REACH * BLK, HALF), BF16),
            pltpu.VMEM((2 * BLK, BLK), BF16),
            pltpu.VMEM((BLK, 2 * BLK), BF16),
            pltpu.VMEM((REACH + 1, NC, ROWS, HALF), BF16),
            pltpu.VMEM((REACH + 1, NC, 2 * BLK, HALF), F32),
            pltpu.VMEM((REACH + 1, 2 * BLK, HALF), F32),
            pltpu.VMEM((2 * BLK, HALF), BF16),
            pltpu.VMEM((NC, BLK, 4 * HALF), BF16),
            pltpu.VMEM((NC, 4 * HALF, 2 * BLK), BF16),
            pltpu.VMEM((BLK, 2 * BLK), F32),
            pltpu.VMEM((BLK, BLK), BF16),
            pltpu.VMEM((BLK, BLK), BF16),
            pltpu.SemaphoreType.DMA((16,)),
            pltpu.SemaphoreType.DMA((96,)),
            pltpu.SemaphoreType.DMA((96,)),
        ],
        compiler_params=pltpu.CompilerParams(collective_id=0, has_side_effects=True, vmem_limit_bytes=56 * 2**20),
        name="hyena",
    )(segment_ids, query, keys, values, filters, out_weight, jnp.asarray(forward), jnp.asarray(backward))


def solution(mesh):
    in_specs = (
        P("ctx", "ch"),
        P("ctx", "ch"),
        P("ctx", "ch"),
        P(None, "ch"),
        P("ctx"),
        P("ch", None),
    )
    return jax.shard_map(on_device, mesh=mesh, in_specs=in_specs, out_specs=P("ctx", "ch"), check_vma=False)
```
